32 devices in a mesh: frame: 8 (over z, y), space: 4 (over x, core).
Axes of the slice: x: 2, y: 2, z: 4, core: 2. Of those that a mesh axis runs over, the one named last changes fastest.
Arguments:
- features: bfloat16 [8, 64, 64, 128], P('frame', None, 'space'), may hold values from -6 to 6
- enc_w: bfloat16 [3, 3, 64, 64], replicated, may hold values from -0.25 to 0.25
- enc_b: float32 [64], replicated, may hold values from -3 to 3
- mix_w: bfloat16 [128, 512], replicated, may hold values from -0.25 to 0.25
- mix_b: float32 [128], replicated, may hold values from -3 to 3
- branch3: bfloat16 [3, 3, 512, 16], P(None, None, 'frame'), may hold values from -0.5 to 0.5
- branch5: bfloat16 [5, 5, 512, 16], P(None, None, 'frame'), may hold values from -0.3125 to 0.3125
- branch7: bfloat16 [7, 7, 512, 16], P(None, None, 'frame'), may hold values from -0.21875 to 0.21875
- branch11: bfloat16 [11, 11, 512, 16], P(None, None, 'frame'), may hold values from -0.125 to 0.125
- branch_b: float32 [4, 512], P(None, 'frame'), may hold values from -3 to 3
- dec_w: bfloat16 [3, 3, 64, 64], replicated, may hold values from -0.25 to 0.25
- dec_b: float32 [64], replicated, may hold values from -3 to 3
Outputs:
- decoded: bfloat16 [8, 64, 64, 128], P('frame', None, 'space')
The draws below stay inside these ranges and needn't reach their ends.
All inputs are finite; a program needn't handle non-finite values.
Results may differ from the reference program's by a relative error of at most 0.019.
Values may be sent and summed in bfloat16 or wider, within the bound.
A program may use at most 64 MiB of HBM per device.

```python
import jax
import jax.numpy as jnp
from jax import lax

C = 64
HID = 128
GROUPS = 8
F = 8
H = 64
W = 128
OUT = 512


def steps_of(stream_key, shape, shards, smallest, largest):
    loudness, own = 1.0, jax.random.fold_in(stream_key, 6)
    for dim, parts in shards:
        steps = jnp.exp(jax.random.uniform(jax.random.fold_in(own, dim), (parts,), jnp.float32, smallest / len(shards), largest / len(shards)))
        loudness = loudness * jnp.repeat(steps, shape[dim] // parts).reshape([-1 if axis == dim else 1 for axis in range(len(shape))])
    return loudness


def gaussian(key, dims, spread, most, pieces=(), dtype=jnp.bfloat16):
    gain = steps_of(key, dims, pieces, -0.22, 0.18) if pieces else 1.0
    values = jax.random.normal(key, dims, jnp.float32) * spread * gain
    return jnp.minimum(jnp.maximum(values, -most), most).astype(dtype)


def setup_inputs(seed: int = 0) -> dict:
    key_list = jax.random.split(jax.random.key(seed), 13)
    features = gaussian(key_list[0], (F, C, H, W), 1.0, 6.0, ((0, 8), (2, 4)))
    enc_w = gaussian(key_list[1], (3, 3, C, C), (9 * C) ** -0.5, 0.25)
    enc_b = gaussian(key_list[2], (C,), 0.5, 3.0, (), jnp.float32)
    mix_w = gaussian(key_list[3], (HID, OUT), OUT ** -0.5, 0.25)
    mix_b = gaussian(key_list[4], (HID,), 0.5, 3.0, (), jnp.float32)
    branch3 = gaussian(key_list[5], (3, 3, OUT, HID // GROUPS), (9 * (HID // GROUPS)) ** -0.5, 0.5, ((2, 8),))
    branch5 = gaussian(key_list[6], (5, 5, OUT, HID // GROUPS), (25 * (HID // GROUPS)) ** -0.5, 0.3125, ((2, 8),))
    branch7 = gaussian(key_list[7], (7, 7, OUT, HID // GROUPS), (49 * (HID // GROUPS)) ** -0.5, 0.21875, ((2, 8),))
    branch11 = gaussian(key_list[8], (11, 11, OUT, HID // GROUPS), (121 * (HID // GROUPS)) ** -0.5, 0.125, ((2, 8),))
    branch_b = gaussian(key_list[9], (4, OUT), 0.5, 3.0, ((1, 8),), jnp.float32)
    dec_w = gaussian(key_list[10], (3, 3, C, C), (9 * C) ** -0.5, 0.25)
    dec_b = gaussian(key_list[11], (C,), 0.5, 3.0, (), jnp.float32)
    return dict(features=features, enc_w=enc_w, enc_b=enc_b, mix_w=mix_w, mix_b=mix_b, branch3=branch3, branch5=branch5, branch7=branch7, branch11=branch11, branch_b=branch_b, dec_w=dec_w, dec_b=dec_b)


def conv_same(values, kernel, width, group_count):
    oihw = jnp.transpose(kernel.astype(jnp.float32), (2, 3, 0, 1))
    half = width // 2
    return lax.conv_general_dilated(values, oihw, (1, 1), ((half, half), (half, half)),
                                    dimension_numbers=("NCHW", "OIHW", "NCHW"),
                                    feature_group_count=group_count,
                                    precision=lax.Precision.HIGHEST)


def reference(features, enc_w, enc_b, mix_w, mix_b, branch3, branch5, branch7, branch11, branch_b, dec_w, dec_b):
    encoded = jax.nn.silu(conv_same(features.astype(jnp.float32), enc_w, 3, 1) + enc_b[None, :, None, None]).astype(jnp.bfloat16)
    frames, channels, row_count, col_count = encoded.shape
    stacked = encoded.reshape(frames * channels, row_count, col_count).astype(jnp.float32)
    hidden = (jnp.einsum("ji,irw->jrw", mix_w.astype(jnp.float32), stacked, precision=lax.Precision.HIGHEST)
              + mix_b[:, None, None]).astype(jnp.bfloat16)
    hidden_batch = hidden.astype(jnp.float32)[None]
    summed = jnp.zeros((frames * channels, row_count, col_count), jnp.float32)
    for branch_index, (width, kernel) in enumerate(((3, branch3), (5, branch5), (7, branch7), (11, branch11))):
        branch = conv_same(hidden_batch, kernel, width, GROUPS)[0] + branch_b[branch_index][:, None, None]
        summed = summed + jnp.where(branch > 0, branch, 0.2 * branch)
    joined = (summed.reshape(frames, channels, row_count, col_count) + encoded.astype(jnp.float32)).astype(jnp.bfloat16)
    return jax.nn.silu(conv_same(joined.astype(jnp.float32), dec_w, 3, 1) + dec_b[None, :, None, None]).astype(jnp.bfloat16)
```

```python
import functools

import jax
import jax.numpy as jnp
from jax import lax
from jax.experimental import pallas as pl
from jax.experimental.pallas import tpu as pltpu
from jax.sharding import PartitionSpec as P

GROUPS = 8
SIZES = (3, 5, 7, 11)
BIG = 11
PAD = BIG // 2
BF16 = jnp.bfloat16
F32 = jnp.float32
MESH = pl.DeviceIdType.MESH


def shifted(x, step):
    if step == 0:
        return x
    width = x.shape[1]
    lane = lax.broadcasted_iota(jnp.int32, x.shape, 1) + step
    rolled = pltpu.roll(x, (-step) % width, 1)
    return jnp.where((lane >= 0) & (lane < width), rolled, 0.0)


def column(row, count, start=0):
    shape = (count, row.shape[1])
    hit = lax.broadcasted_iota(jnp.int32, shape, 1) == (
        lax.broadcasted_iota(jnp.int32, shape, 0) + start
    )
    return jnp.sum(jnp.where(hit, jnp.broadcast_to(row, shape), 0.0), axis=1, keepdims=True)


def silu(v):
    return v / (1.0 + jnp.exp(-v))


def kernel(
    frames,
    spaces,
    feat,
    enc_w,
    enc_b,
    mix_w,
    mix_b,
    branch3,
    branch5,
    branch7,
    branch11,
    branch_b,
    dec_w,
    dec_b,
    out,
    w3e,
    w3d,
    wbig,
    raw3,
    raw5,
    raw7,
    raw11,
    s3,
    s11,
    enc,
    part,
    arrived,
    hid,
    joined,
    x_halo,
    h_halo,
    j_halo,
    load_sem,
    x_send,
    x_recv,
    p_send,
    p_recv,
    h_send,
    h_recv,
    j_send,
    j_recv,
):
    rows, channels, width = feat.shape
    inner = part.shape[2]
    out_channels = frames * channels
    frame, space = lax.axis_index("frame"), lax.axis_index("space")
    above, below = space > 0, space < spaces - 1

    raws = (raw3, raw5, raw7, raw11)
    loads = [
        pltpu.make_async_copy(source, target, load_sem.at[n])
        for n, (source, target) in enumerate(
            zip((branch3, branch5, branch7, branch11), raws)
        )
    ]
    for load in loads:
        load.start()

    barrier = pltpu.get_barrier_semaphore()

    def greet(device):
        pl.semaphore_signal(barrier, inc=1, device_id=device, device_id_type=MESH)

    @pl.when(above)
    def _():
        greet({"space": space - 1})

    @pl.when(below)
    def _():
        greet({"space": space + 1})

    for step in range(1, frames):
        greet({"frame": lax.rem(frame + step, frames)})

    def up(first, halo, send, recv):
        return pltpu.make_async_remote_copy(
            src_ref=first,
            dst_ref=halo.at[1],
            send_sem=send.at[1],
            recv_sem=recv.at[1],
            device_id={"space": space - 1},
            device_id_type=MESH,
        )

    def down(last, halo, send, recv):
        return pltpu.make_async_remote_copy(
            src_ref=last,
            dst_ref=halo.at[0],
            send_sem=send.at[0],
            recv_sem=recv.at[0],
            device_id={"space": space + 1},
            device_id_type=MESH,
        )

    def edges_start(first, last, *rest):
        @pl.when(above)
        def _():
            up(first, *rest).start()

        @pl.when(below)
        def _():
            down(last, *rest).start()

    def edges_sent(first, last, *rest):
        @pl.when(above)
        def _():
            up(first, *rest).wait_send()

        @pl.when(below)
        def _():
            down(last, *rest).wait_send()

    def put3(row, x):
        x = x.astype(F32)
        for tap in range(3):
            s3[row, tap * channels : (tap + 1) * channels, :] = shifted(x, tap - 1).astype(BF16)

    def edges3(first, last, halo, send, recv):
        @pl.when(above)
        def _():
            down(last, halo, send, recv).wait_recv()
            put3(0, halo[0])

        @pl.when(jnp.logical_not(above))
        def _():
            s3[0] = jnp.zeros((3 * channels, width), BF16)

        @pl.when(below)
        def _():
            up(first, halo, send, recv).wait_recv()
            put3(rows + 1, halo[1])

        @pl.when(jnp.logical_not(below))
        def _():
            s3[rows + 1] = jnp.zeros((3 * channels, width), BF16)

    def conv3(weight, bias, row):
        depth = 9 * channels
        window = jnp.concatenate(
            [s3[pl.ds(row + h, 3)].reshape(depth, width) for h in range(2)], axis=1
        )
        return silu(jnp.dot(weight[...], window, preferred_element_type=F32) + bias).astype(BF16)

    def lay3(source, target):
        flat = [source[tap // 3, tap % 3] for tap in range(9)]
        for pair in range(4):
            target[:, pair * 2 * channels : (pair + 1) * 2 * channels] = jnp.concatenate(
                flat[2 * pair : 2 * pair + 2], axis=1
            )
        target[:, 8 * channels :] = flat[8]

    lay3(enc_w, w3e)
    enc_col = column(enc_b[...], channels)

    per_block = 128 // channels
    block = mix_w[:, pl.ds(pl.multiple_of((frame // per_block) * 128, 128), 128)]
    own_mix = block[:, :channels]
    for piece in range(1, per_block):
        own_mix = jnp.where(
            lax.rem(frame, per_block) == piece,
            block[:, piece * channels : (piece + 1) * channels],
            own_mix,
        )

    pl.semaphore_wait(
        barrier, frames - 1 + above.astype(jnp.int32) + below.astype(jnp.int32)
    )

    x_args = (feat.at[0], feat.at[rows - 1], x_halo, x_send, x_recv)
    edges_start(*x_args)

    @pl.loop(0, rows)
    def _(row):
        put3(row + 1, feat[row])

    def encode(row):
        e = conv3(w3e, enc_col, row)
        p = jnp.dot(own_mix, e, preferred_element_type=F32).astype(BF16)
        for h in range(2):
            enc[row + h] = e[:, h * width : (h + 1) * width]
            part[:, row + h] = p[:, h * width : (h + 1) * width].reshape(
                p.shape[0] // inner, inner, width
            )

    @pl.loop(1, rows // 2 - 1)
    def _(pair):
        encode(2 * pair)

    edges3(*x_args)
    encode(0)
    encode(rows - 2)

    per_group = out_channels // GROUPS

    def group_of(index):
        return (index * channels) // per_group

    def share(step):
        peer = lax.rem(frame + step, frames)
        return pltpu.make_async_remote_copy(
            src_ref=part.at[group_of(peer)],
            dst_ref=arrived.at[step - 1],
            send_sem=p_send.at[step - 1],
            recv_sem=p_recv.at[step - 1],
            device_id={"frame": peer},
            device_id_type=MESH,
        )

    for step in range(1, frames):
        share(step).start()

    lay3(dec_w, w3d)
    dec_col = column(dec_b[...], channels)
    branch_col = jnp.concatenate(
        [column(branch_b[n : n + 1, :], channels) for n in range(4)], axis=0
    )
    mix_col = column(mix_b[...], inner, group_of(frame) * inner)
    for load in loads:
        load.wait()
    taps = BIG * BIG
    many = 128 // inner
    empty = jnp.zeros((channels, inner), BF16)
    for n, (size, raw) in enumerate(zip(SIZES, raws)):
        skip = PAD - size // 2
        for first in range(0, taps, many):
            pieces, used = [], False
            for tap in range(first, min(first + many, taps)):
                a, b = tap // BIG - skip, tap % BIG - skip
                inside = 0 <= a < size and 0 <= b < size
                used = used or inside
                pieces.append(raw[a, b] if inside else empty)
            count = len(pieces) * inner
            value = (
                jnp.concatenate(pieces, axis=1) if used else jnp.zeros((channels, count), BF16)
            )
            wbig[n * channels : (n + 1) * channels, first * inner : first * inner + count] = value

    total = part[group_of(frame)].astype(F32)
    for step in range(1, frames):
        share(step).wait_recv()
        total = total + arrived[step - 1].astype(F32)
    total = (total + mix_col[None]).astype(BF16)
    hid[...] = total
    h_args = (hid.at[0:PAD], hid.at[rows - PAD : rows], h_halo, h_send, h_recv)
    edges_start(*h_args)

    def put11(row, x):
        count = x.shape[0]
        x = x.astype(F32).reshape(count * inner, width)
        for tap in range(BIG):
            s11[row : row + count, tap * inner : (tap + 1) * inner, :] = (
                shifted(x, tap - PAD).astype(BF16).reshape(count, inner, width)
            )

    put11(PAD, total)

    def mixed(row):
        depth = BIG * BIG * inner
        window = jnp.concatenate(
            [s11[pl.ds(row + h, BIG)].reshape(depth, width) for h in range(2)], axis=1
        )
        pre = jnp.dot(wbig[...], window, preferred_element_type=F32) + branch_col
        pre = jnp.where(pre > 0, pre, 0.2 * pre)
        pre = pre.reshape(4, channels, 2 * width)
        total = pre[0] + pre[1] + pre[2] + pre[3]
        for h in range(2):
            whole = (total[:, h * width : (h + 1) * width] + enc[row + h].astype(F32)).astype(BF16)
            joined[row + h] = whole
            put3(row + h + 1, whole)

    low = (PAD + 1) // 2
    high = (rows - PAD) // 2

    @pl.loop(low, high)
    def _(pair):
        mixed(2 * pair)

    nothing = jnp.zeros((PAD, BIG * inner, width), BF16)

    @pl.when(above)
    def _():
        down(h_args[1], *h_args[2:]).wait_recv()
        put11(0, h_halo[0])

    @pl.when(jnp.logical_not(above))
    def _():
        s11[0:PAD] = nothing

    @pl.when(below)
    def _():
        up(h_args[0], *h_args[2:]).wait_recv()
        put11(rows + PAD, h_halo[1])

    @pl.when(jnp.logical_not(below))
    def _():
        s11[rows + PAD : rows + 2 * PAD] = nothing

    @pl.loop(0, 2)
    def _(side):
        mixed(side * (rows - 2))

    j_args = (joined.at[0], joined.at[rows - 1], j_halo, j_send, j_recv)
    edges_start(*j_args)

    @pl.loop(1, low)
    def _(pair):
        mixed(2 * pair)

    @pl.loop(high, rows // 2 - 1)
    def _(pair):
        mixed(2 * pair)

    def decode(row):
        d = conv3(w3d, dec_col, row)
        for h in range(2):
            out[row + h] = d[:, h * width : (h + 1) * width]

    @pl.loop(1, rows // 2 - 1)
    def _(pair):
        decode(2 * pair)

    edges3(*j_args)
    decode(0)
    decode(rows - 2)

    edges_sent(*x_args)
    edges_sent(*h_args)
    edges_sent(*j_args)
    for step in range(1, frames):
        share(step).wait_send()


def per_device(
    frames,
    spaces,
    features,
    enc_w,
    enc_b,
    mix_w,
    mix_b,
    branch3,
    branch5,
    branch7,
    branch11,
    branch_b,
    dec_w,
    dec_b,
):
    channels, rows, width = features.shape[1:]
    inner = mix_w.shape[0] // GROUPS
    vmem = pl.BlockSpec(memory_space=pltpu.VMEM)
    hbm = pl.BlockSpec(memory_space=pl.ANY)
    strip = (rows, channels, width)
    pair = pltpu.SemaphoreType.DMA((2,))
    many = pltpu.SemaphoreType.DMA((frames - 1,))
    decoded = pl.pallas_call(
        functools.partial(kernel, frames, spaces),
        out_shape=jax.ShapeDtypeStruct(strip, BF16),
        in_specs=[vmem] * 5 + [hbm] * 4 + [vmem] * 3,
        out_specs=vmem,
        scratch_shapes=[
            pltpu.VMEM((channels, 9 * channels), BF16),
            pltpu.VMEM((channels, 9 * channels), BF16),
            pltpu.VMEM((4 * channels, BIG * BIG * inner), BF16),
            pltpu.VMEM(branch3.shape, BF16),
            pltpu.VMEM(branch5.shape, BF16),
            pltpu.VMEM(branch7.shape, BF16),
            pltpu.VMEM(branch11.shape, BF16),
            pltpu.VMEM((rows + 2, 3 * channels, width), BF16),
            pltpu.VMEM((rows + 2 * PAD, BIG * inner, width), BF16),
            pltpu.VMEM(strip, BF16),
            pltpu.VMEM((GROUPS, rows, inner, width), BF16),
            pltpu.VMEM((frames - 1, rows, inner, width), BF16),
            pltpu.VMEM((rows, inner, width), BF16),
            pltpu.VMEM(strip, BF16),
            pltpu.VMEM((2, channels, width), BF16),
            pltpu.VMEM((2, PAD, inner, width), BF16),
            pltpu.VMEM((2, channels, width), BF16),
            pltpu.SemaphoreType.DMA((4,)),
            pair,
            pair,
            many,
            many,
            pair,
            pair,
            pair,
            pair,
        ],
        compiler_params=pltpu.CompilerParams(
            collective_id=0, has_side_effects=True, vmem_limit_bytes=40 * 2**20
        ),
    )(
        jnp.transpose(features[0], (1, 0, 2)),
        enc_w,
        enc_b[None],
        mix_w,
        mix_b[None],
        branch3,
        branch5,
        branch7,
        branch11,
        branch_b,
        dec_w,
        dec_b[None],
    )
    return jnp.transpose(decoded, (1, 0, 2))[None]


def solution(mesh):
    placed = (
        P("frame", None, "space", None),
        P(),
        P(),
        P(),
        P(),
        P(None, None, "frame", None),
        P(None, None, "frame", None),
        P(None, None, "frame", None),
        P(None, None, "frame", None),
        P(None, "frame"),
        P(),
        P(),
    )
    return jax.shard_map(
        functools.partial(per_device, mesh.shape["frame"], mesh.shape["space"]),
        mesh=mesh,
        in_specs=placed,
        out_specs=P("frame", None, "space", None),
        check_vma=False,
    )
```

```python
import functools

import jax
import jax.numpy as jnp
from jax import lax
from jax.experimental import pallas as pl
from jax.experimental.pallas import tpu as pltpu
from jax.sharding import PartitionSpec as P

GROUPS = 8
SIZES = (3, 5, 7, 11)
BIG = 11
PAD = BIG // 2
BF16 = jnp.bfloat16
F32 = jnp.float32
MESH = pl.DeviceIdType.MESH


def shifted(x, step):
    if step == 0:
        return x
    width = x.shape[1]
    lane = lax.broadcasted_iota(jnp.int32, x.shape, 1) + step
    rolled = pltpu.roll(x, (-step) % width, 1)
    return jnp.where((lane >= 0) & (lane < width), rolled, 0.0)


def column(row, count, start=0):
    shape = (count, row.shape[1])
    hit = lax.broadcasted_iota(jnp.int32, shape, 1) == (
        lax.broadcasted_iota(jnp.int32, shape, 0) + start
    )
    return jnp.sum(jnp.where(hit, jnp.broadcast_to(row, shape), 0.0), axis=1, keepdims=True)


def silu(v):
    return v / (1.0 + jnp.exp(-v))


def kernel(
    frames,
    spaces,
    features,
    enc_w_all,
    mix_w,
    branch3,
    branch5,
    branch7,
    branch11,
    dec_w_all,
    enc_b,
    mix_b,
    branch_b,
    dec_b,
    out,
    planes,
    feat,
    enc_w,
    mix_block,
    dec_w,
    wt,
    w3e,
    w3d,
    wbig,
    raw3,
    raw5,
    raw7,
    raw11,
    s3,
    s11,
    enc,
    part,
    arrived,
    hid,
    joined,
    x_halo,
    h_halo,
    j_halo,
    load_sem,
    x_send,
    x_recv,
    p_send,
    p_recv,
    h_send,
    h_recv,
    j_send,
    j_recv,
):
    rows, channels, width = feat.shape
    inner = part.shape[2]
    out_channels = frames * channels
    frame, space = lax.axis_index("frame"), lax.axis_index("space")
    above, below = space > 0, space < spaces - 1

    per_block = 128 // channels
    mix_columns = pl.ds(pl.multiple_of((frame // per_block) * 128, 128), 128)
    raws = (raw3, raw5, raw7, raw11)
    loads = [
        pltpu.make_async_copy(source, target, load_sem.at[n])
        for n, (source, target) in enumerate(
            (
                (features.at[0], planes),
                (enc_w_all, enc_w),
                (mix_w.at[:, mix_columns], mix_block),
                (dec_w_all, dec_w),
                (branch3, raw3),
                (branch5, raw5),
                (branch7, raw7),
                (branch11, raw11),
            )
        )
    ]
    for load in loads:
        load.start()

    barrier = pltpu.get_barrier_semaphore()

    def greet(device):
        pl.semaphore_signal(barrier, inc=1, device_id=device, device_id_type=MESH)

    @pl.when(above)
    def _():
        greet({"space": space - 1})

    @pl.when(below)
    def _():
        greet({"space": space + 1})

    for step in range(1, frames):
        greet({"frame": lax.rem(frame + step, frames)})

    def up(first, halo, send, recv):
        return pltpu.make_async_remote_copy(
            src_ref=first,
            dst_ref=halo.at[1],
            send_sem=send.at[1],
            recv_sem=recv.at[1],
            device_id={"space": space - 1},
            device_id_type=MESH,
        )

    def down(last, halo, send, recv):
        return pltpu.make_async_remote_copy(
            src_ref=last,
            dst_ref=halo.at[0],
            send_sem=send.at[0],
            recv_sem=recv.at[0],
            device_id={"space": space + 1},
            device_id_type=MESH,
        )

    def edges_start(first, last, *rest):
        @pl.when(above)
        def _():
            up(first, *rest).start()

        @pl.when(below)
        def _():
            down(last, *rest).start()

    def edges_sent(first, last, *rest):
        @pl.when(above)
        def _():
            up(first, *rest).wait_send()

        @pl.when(below)
        def _():
            down(last, *rest).wait_send()

    def put3(row, x):
        x = x.astype(F32)
        for tap in range(3):
            s3[row, tap * channels : (tap + 1) * channels, :] = shifted(x, tap - 1).astype(BF16)

    def edges3(first, last, halo, send, recv):
        @pl.when(above)
        def _():
            down(last, halo, send, recv).wait_recv()
            put3(0, halo[0])

        @pl.when(jnp.logical_not(above))
        def _():
            s3[0] = jnp.zeros((3 * channels, width), BF16)

        @pl.when(below)
        def _():
            up(first, halo, send, recv).wait_recv()
            put3(rows + 1, halo[1])

        @pl.when(jnp.logical_not(below))
        def _():
            s3[rows + 1] = jnp.zeros((3 * channels, width), BF16)

    def conv3(weight, bias, row):
        depth = 9 * channels
        window = jnp.concatenate(
            [s3[pl.ds(row + h, 3)].reshape(depth, width) for h in range(2)], axis=1
        )
        return silu(jnp.dot(weight[...], window, preferred_element_type=F32) + bias).astype(BF16)

    def lay3(source, target):
        flat = [source[tap // 3, tap % 3] for tap in range(9)]
        for pair in range(4):
            target[:, pair * 2 * channels : (pair + 1) * 2 * channels] = jnp.concatenate(
                flat[2 * pair : 2 * pair + 2], axis=1
            )
        target[:, 8 * channels :] = flat[8]

    loads[0].wait()
    feat[...] = jnp.transpose(planes[...], (1, 0, 2))
    enc_col = column(enc_b[...], channels)
    loads[1].wait()
    lay3(enc_w, w3e)
    loads[2].wait()
    block = mix_block[...]
    own_mix = block[:, :channels]
    for piece in range(1, per_block):
        own_mix = jnp.where(
            lax.rem(frame, per_block) == piece,
            block[:, piece * channels : (piece + 1) * channels],
            own_mix,
        )

    pl.semaphore_wait(
        barrier, frames - 1 + above.astype(jnp.int32) + below.astype(jnp.int32)
    )

    x_args = (feat.at[0], feat.at[rows - 1], x_halo, x_send, x_recv)
    edges_start(*x_args)

    @pl.loop(0, rows)
    def _(row):
        put3(row + 1, feat[row])

    def encode(row):
        e = conv3(w3e, enc_col, row)
        p = jnp.dot(own_mix, e, preferred_element_type=F32).astype(BF16)
        for h in range(2):
            enc[row + h] = e[:, h * width : (h + 1) * width]
            part[:, row + h] = p[:, h * width : (h + 1) * width].reshape(
                p.shape[0] // inner, inner, width
            )

    @pl.loop(1, rows // 2 - 1)
    def _(pair):
        encode(2 * pair)

    edges3(*x_args)
    encode(0)
    encode(rows - 2)

    per_group = out_channels // GROUPS

    def group_of(index):
        return (index * channels) // per_group

    def share(step):
        peer = lax.rem(frame + step, frames)
        return pltpu.make_async_remote_copy(
            src_ref=part.at[group_of(peer)],
            dst_ref=arrived.at[step - 1],
            send_sem=p_send.at[step - 1],
            recv_sem=p_recv.at[step - 1],
            device_id={"frame": peer},
            device_id_type=MESH,
        )

    for step in range(1, frames):
        share(step).start()

    dec_col = column(dec_b[...], channels)
    branch_col = jnp.concatenate(
        [column(branch_b[n : n + 1, :], channels) for n in range(4)], axis=0
    )
    mix_col = column(mix_b[...], inner, group_of(frame) * inner)
    for load in loads[3:]:
        load.wait()
    lay3(dec_w, w3d)
    for a in range(BIG):
        blocks = []
        for size, raw in zip(SIZES, raws):
            skip = PAD - size // 2
            if skip <= a < skip + size:
                some = raw[a - skip].reshape(size * inner, channels)
                edge = [jnp.zeros((skip * inner, channels), BF16)] if skip else []
                blocks.append(jnp.concatenate(edge + [some] + edge, axis=0))
            else:
                blocks.append(jnp.zeros((BIG * inner, channels), BF16))
        wt[a * BIG * inner : (a + 1) * BIG * inner, :] = jnp.concatenate(blocks, axis=1)
    taps = BIG * BIG * inner
    for first in range(0, taps, 128):
        last = min(first + 128, taps)
        wbig[:, first:last] = wt[first:last, :].T

    total = part[group_of(frame)].astype(F32)
    for step in range(1, frames):
        share(step).wait_recv()
        total = total + arrived[step - 1].astype(F32)
    total = (total + mix_col[None]).astype(BF16)
    hid[...] = total
    h_args = (hid.at[0:PAD], hid.at[rows - PAD : rows], h_halo, h_send, h_recv)
    edges_start(*h_args)

    def put11(row, x):
        count = x.shape[0]
        x = x.astype(F32).reshape(count * inner, width)
        for tap in range(BIG):
            s11[row : row + count, tap * inner : (tap + 1) * inner, :] = (
                shifted(x, tap - PAD).astype(BF16).reshape(count, inner, width)
            )

    put11(PAD, total)

    def mixed(row):
        depth = BIG * BIG * inner
        window = jnp.concatenate(
            [s11[pl.ds(row + h, BIG)].reshape(depth, width) for h in range(2)], axis=1
        )
        pre = jnp.dot(wbig[...], window, preferred_element_type=F32) + branch_col
        pre = jnp.where(pre > 0, pre, 0.2 * pre)
        pre = pre.reshape(4, channels, 2 * width)
        total = pre[0] + pre[1] + pre[2] + pre[3]
        for h in range(2):
            whole = (total[:, h * width : (h + 1) * width] + enc[row + h].astype(F32)).astype(BF16)
            joined[row + h] = whole
            put3(row + h + 1, whole)

    low = (PAD + 1) // 2
    high = (rows - PAD) // 2

    @pl.loop(low, high)
    def _(pair):
        mixed(2 * pair)

    nothing = jnp.zeros((PAD, BIG * inner, width), BF16)

    @pl.when(above)
    def _():
        down(h_args[1], *h_args[2:]).wait_recv()
        put11(0, h_halo[0])

    @pl.when(jnp.logical_not(above))
    def _():
        s11[0:PAD] = nothing

    @pl.when(below)
    def _():
        up(h_args[0], *h_args[2:]).wait_recv()
        put11(rows + PAD, h_halo[1])

    @pl.when(jnp.logical_not(below))
    def _():
        s11[rows + PAD : rows + 2 * PAD] = nothing

    @pl.loop(0, 2)
    def _(side):
        mixed(side * (rows - 2))

    j_args = (joined.at[0], joined.at[rows - 1], j_halo, j_send, j_recv)
    edges_start(*j_args)

    @pl.loop(1, low)
    def _(pair):
        mixed(2 * pair)

    @pl.loop(high, rows // 2 - 1)
    def _(pair):
        mixed(2 * pair)

    def decode(row):
        d = conv3(w3d, dec_col, row)
        for h in range(2):
            out[row + h] = d[:, h * width : (h + 1) * width]

    @pl.loop(1, rows // 2 - 1)
    def _(pair):
        decode(2 * pair)

    edges3(*j_args)
    decode(0)
    decode(rows - 2)

    edges_sent(*x_args)
    edges_sent(*h_args)
    edges_sent(*j_args)
    for step in range(1, frames):
        share(step).wait_send()


def per_device(
    frames,
    spaces,
    features,
    enc_w,
    enc_b,
    mix_w,
    mix_b,
    branch3,
    branch5,
    branch7,
    branch11,
    branch_b,
    dec_w,
    dec_b,
):
    channels, rows, width = features.shape[1:]
    inner = mix_w.shape[0] // GROUPS
    branches = [jnp.transpose(w, (0, 1, 3, 2)) for w in (branch3, branch5, branch7, branch11)]
    vmem = pl.BlockSpec(memory_space=pltpu.VMEM)
    hbm = pl.BlockSpec(memory_space=pltpu.HBM)
    strip = (rows, channels, width)
    pair = pltpu.SemaphoreType.DMA((2,))
    many = pltpu.SemaphoreType.DMA((frames - 1,))
    decoded = pl.pallas_call(
        functools.partial(kernel, frames, spaces),
        out_shape=jax.ShapeDtypeStruct(strip, BF16),
        in_specs=[hbm] * 8 + [vmem] * 4,
        out_specs=vmem,
        scratch_shapes=[
            pltpu.VMEM((channels, rows, width), BF16),
            pltpu.VMEM(strip, BF16),
            pltpu.VMEM(enc_w.shape, BF16),
            pltpu.VMEM((mix_w.shape[0], 128), BF16),
            pltpu.VMEM(dec_w.shape, BF16),
            pltpu.VMEM((BIG * BIG * inner, 4 * channels), BF16),
            pltpu.VMEM((channels, 9 * channels), BF16),
            pltpu.VMEM((channels, 9 * channels), BF16),
            pltpu.VMEM((4 * channels, BIG * BIG * inner), BF16),
            pltpu.VMEM(branches[0].shape, BF16),
            pltpu.VMEM(branches[1].shape, BF16),
            pltpu.VMEM(branches[2].shape, BF16),
            pltpu.VMEM(branches[3].shape, BF16),
            pltpu.VMEM((rows + 2, 3 * channels, width), BF16),
            pltpu.VMEM((rows + 2 * PAD, BIG * inner, width), BF16),
            pltpu.VMEM(strip, BF16),
            pltpu.VMEM((GROUPS, rows, inner, width), BF16),
            pltpu.VMEM((frames - 1, rows, inner, width), BF16),
            pltpu.VMEM((rows, inner, width), BF16),
            pltpu.VMEM(strip, BF16),
            pltpu.VMEM((2, channels, width), BF16),
            pltpu.VMEM((2, PAD, inner, width), BF16),
            pltpu.VMEM((2, channels, width), BF16),
            pltpu.SemaphoreType.DMA((8,)),
            pair,
            pair,
            many,
            many,
            pair,
            pair,
            pair,
            pair,
        ],
        compiler_params=pltpu.CompilerParams(
            collective_id=0, has_side_effects=True, vmem_limit_bytes=62 * 2**20
        ),
    )(
        features,
        enc_w,
        mix_w,
        *branches,
        dec_w,
        enc_b[None],
        mix_b[None],
        branch_b,
        dec_b[None],
    )
    return jnp.transpose(decoded, (1, 0, 2))[None]


def solution(mesh):
    placed = (
        P("frame", None, "space", None),
        P(),
        P(),
        P(),
        P(),
        P(None, None, "frame", None),
        P(None, None, "frame", None),
        P(None, None, "frame", None),
        P(None, None, "frame", None),
        P(None, "frame"),
        P(),
        P(),
    )
    return jax.shard_map(
        functools.partial(per_device, mesh.shape["frame"], mesh.shape["space"]),
        mesh=mesh,
        in_specs=placed,
        out_specs=P("frame", None, "space", None),
        check_vma=False,
    )
```

```python
import functools

import jax
import jax.numpy as jnp
from jax import lax
from jax.experimental import pallas as pl
from jax.experimental.pallas import tpu as pltpu
from jax.sharding import PartitionSpec as P

GROUPS = 8
SIZES = (3, 5, 7, 11)
BIG = 11
PAD = BIG // 2
BF16 = jnp.bfloat16
F32 = jnp.float32
MESH = pl.DeviceIdType.MESH


def shifted(x, step):
    if step == 0:
        return x
    width = x.shape[1]
    lane = lax.broadcasted_iota(jnp.int32, x.shape, 1) + step
    rolled = pltpu.roll(x, (-step) % width, 1)
    return jnp.where((lane >= 0) & (lane < width), rolled, 0.0)


def column(row, count, start=0):
    shape = (count, row.shape[1])
    hit = lax.broadcasted_iota(jnp.int32, shape, 1) == (
        lax.broadcasted_iota(jnp.int32, shape, 0) + start
    )
    return jnp.sum(jnp.where(hit, jnp.broadcast_to(row, shape), 0.0), axis=1, keepdims=True)


def silu(v):
    return v / (1.0 + jnp.exp(-v))


def kernel(
    frames,
    spaces,
    features,
    enc_w_all,
    mix_w,
    branch3,
    branch5,
    branch7,
    branch11,
    dec_w_all,
    enc_b,
    mix_b,
    branch_b,
    dec_b,
    out,
    planes,
    feat,
    enc_w,
    mix_block,
    dec_w,
    wt,
    w3e,
    w3d,
    wbig,
    raw3,
    raw5,
    raw7,
    raw11,
    s3,
    s11,
    enc,
    part,
    arrived,
    hid,
    joined,
    x_halo,
    h_halo,
    j_halo,
    load_sem,
    x_send,
    x_recv,
    p_send,
    p_recv,
    h_send,
    h_recv,
    j_send,
    j_recv,
):
    rows, channels, width = feat.shape
    inner = part.shape[2]
    out_channels = frames * channels
    frame, space = lax.axis_index("frame"), lax.axis_index("space")
    above, below = space > 0, space < spaces - 1

    per_block = 128 // channels
    mix_columns = pl.ds(pl.multiple_of((frame // per_block) * 128, 128), 128)
    raws = (raw3, raw5, raw7, raw11)
    loads = [
        pltpu.make_async_copy(source, target, load_sem.at[n])
        for n, (source, target) in enumerate(
            (
                (features.at[0], planes),
                (enc_w_all, enc_w),
                (mix_w.at[:, mix_columns], mix_block),
                (dec_w_all, dec_w),
                (branch3, raw3),
                (branch5, raw5),
                (branch7, raw7),
                (branch11, raw11),
            )
        )
    ]
    for load in loads:
        load.start()

    barrier = pltpu.get_barrier_semaphore()

    def greet(device):
        pl.semaphore_signal(barrier, inc=1, device_id=device, device_id_type=MESH)

    @pl.when(above)
    def _():
        greet({"space": space - 1})

    @pl.when(below)
    def _():
        greet({"space": space + 1})

    for step in range(1, frames):
        greet({"frame": lax.rem(frame + step, frames)})

    def up(first, halo, send, recv):
        return pltpu.make_async_remote_copy(
            src_ref=first,
            dst_ref=halo.at[1],
            send_sem=send.at[1],
            recv_sem=recv.at[1],
            device_id={"space": space - 1},
            device_id_type=MESH,
        )

    def down(last, halo, send, recv):
        return pltpu.make_async_remote_copy(
            src_ref=last,
            dst_ref=halo.at[0],
            send_sem=send.at[0],
            recv_sem=recv.at[0],
            device_id={"space": space + 1},
            device_id_type=MESH,
        )

    def edges_start(first, last, *rest):
        @pl.when(above)
        def _():
            up(first, *rest).start()

        @pl.when(below)
        def _():
            down(last, *rest).start()

    def edges_sent(first, last, *rest):
        @pl.when(above)
        def _():
            up(first, *rest).wait_send()

        @pl.when(below)
        def _():
            down(last, *rest).wait_send()

    def put3(row, x):
        x = x.astype(F32)
        for tap in range(3):
            s3[row, tap * channels : (tap + 1) * channels, :] = shifted(x, tap - 1).astype(BF16)

    def edges3(first, last, halo, send, recv):
        @pl.when(above)
        def _():
            down(last, halo, send, recv).wait_recv()
            put3(0, halo[0])

        @pl.when(jnp.logical_not(above))
        def _():
            s3[0] = jnp.zeros((3 * channels, width), BF16)

        @pl.when(below)
        def _():
            up(first, halo, send, recv).wait_recv()
            put3(rows + 1, halo[1])

        @pl.when(jnp.logical_not(below))
        def _():
            s3[rows + 1] = jnp.zeros((3 * channels, width), BF16)

    def conv3(weight, bias, row):
        depth = 9 * channels
        window = jnp.concatenate(
            [s3[pl.ds(row + h, 3)].reshape(depth, width) for h in range(2)], axis=1
        )
        return silu(jnp.dot(weight[...], window, preferred_element_type=F32) + bias).astype(BF16)

    def lay3(source, target):
        flat = [source[tap // 3, tap % 3] for tap in range(9)]
        for pair in range(4):
            target[:, pair * 2 * channels : (pair + 1) * 2 * channels] = jnp.concatenate(
                flat[2 * pair : 2 * pair + 2], axis=1
            )
        target[:, 8 * channels :] = flat[8]

    loads[0].wait()
    feat[...] = jnp.transpose(planes[...], (1, 0, 2))
    enc_col = column(enc_b[...], channels)
    loads[1].wait()
    lay3(enc_w, w3e)
    loads[2].wait()
    block = mix_block[...]
    own_mix = block[:, :channels]
    for piece in range(1, per_block):
        own_mix = jnp.where(
            lax.rem(frame, per_block) == piece,
            block[:, piece * channels : (piece + 1) * channels],
            own_mix,
        )

    @pl.loop(0, rows)
    def _(row):
        put3(row + 1, feat[row])

    near = [*range(2, PAD), *range(rows - PAD, rows - 2)]
    edge = [0, 1, rows - 2, rows - 1]
    middle = [*range(PAD, rows - PAD)]
    place = {row: n for n, row in enumerate(near + edge + middle)}
    chunks = (
        (0, len(near)),
        (len(near), len(edge)),
        (len(near) + len(edge), len(middle)),
    )

    def encode(row):
        e = conv3(w3e, enc_col, row)
        p = jnp.dot(own_mix, e, preferred_element_type=F32).astype(BF16)
        for h in range(2):
            enc[row + h] = e[:, h * width : (h + 1) * width]
            part[:, place[row + h]] = p[:, h * width : (h + 1) * width].reshape(
                p.shape[0] // inner, inner, width
            )

    for row in range(2, rows - 2, 2):
        encode(row)

    pl.semaphore_wait(
        barrier, frames - 1 + above.astype(jnp.int32) + below.astype(jnp.int32)
    )

    x_args = (feat.at[0], feat.at[rows - 1], x_halo, x_send, x_recv)
    edges_start(*x_args)

    per_group = out_channels // GROUPS

    def group_of(index):
        return (index * channels) // per_group

    def share(step, chunk):
        peer = lax.rem(frame + step, frames)
        first, count = chunks[chunk]
        flight = chunk * (frames - 1) + step - 1
        return pltpu.make_async_remote_copy(
            src_ref=part.at[group_of(peer), first : first + count],
            dst_ref=arrived.at[step - 1, first : first + count],
            send_sem=p_send.at[flight],
            recv_sem=p_recv.at[flight],
            device_id={"frame": peer},
            device_id_type=MESH,
        )

    def summed(chunk):
        first, count = chunks[chunk]
        total = part[group_of(frame), first : first + count].astype(F32)
        for step in range(1, frames):
            share(step, chunk).wait_recv()
            total = total + arrived[step - 1, first : first + count].astype(F32)
        return (total + mix_col[None]).astype(BF16)

    for step in range(1, frames):
        share(step, 0).start()

    edges3(*x_args)
    encode(0)
    encode(rows - 2)
    for chunk in (1, 2):
        for step in range(1, frames):
            share(step, chunk).start()

    dec_col = column(dec_b[...], channels)
    branch_col = jnp.concatenate(
        [column(branch_b[n : n + 1, :], channels) for n in range(4)], axis=0
    )
    mix_col = column(mix_b[...], inner, group_of(frame) * inner)
    for load in loads[3:]:
        load.wait()
    lay3(dec_w, w3d)
    for a in range(BIG):
        blocks = []
        for size, raw in zip(SIZES, raws):
            skip = PAD - size // 2
            if skip <= a < skip + size:
                some = raw[a - skip].reshape(size * inner, channels)
                edge = [jnp.zeros((skip * inner, channels), BF16)] if skip else []
                blocks.append(jnp.concatenate(edge + [some] + edge, axis=0))
            else:
                blocks.append(jnp.zeros((BIG * inner, channels), BF16))
        wt[a * BIG * inner : (a + 1) * BIG * inner, :] = jnp.concatenate(blocks, axis=1)
    taps = BIG * BIG * inner
    for first in range(0, taps, 128):
        last = min(first + 128, taps)
        wbig[:, first:last] = wt[first:last, :].T

    some, outer = summed(0), summed(1)
    half = len(near) // 2
    hid[0] = jnp.concatenate([outer[:2], some[:half]], axis=0)
    hid[1] = jnp.concatenate([some[half:], outer[2:]], axis=0)
    h_args = (hid.at[0], hid.at[1], h_halo, h_send, h_recv)
    edges_start(*h_args)

    def put11(row, x):
        count = x.shape[0]
        x = x.astype(F32).reshape(count * inner, width)
        for tap in range(BIG):
            s11[row : row + count, tap * inner : (tap + 1) * inner, :] = (
                shifted(x, tap - PAD).astype(BF16).reshape(count, inner, width)
            )

    put11(PAD, hid[0])
    put11(rows, hid[1])
    put11(2 * PAD, summed(2))

    def mixed(row):
        depth = BIG * BIG * inner
        window = jnp.concatenate(
            [s11[pl.ds(row + h, BIG)].reshape(depth, width) for h in range(2)], axis=1
        )
        pre = jnp.dot(wbig[...], window, preferred_element_type=F32) + branch_col
        pre = jnp.where(pre > 0, pre, 0.2 * pre)
        pre = pre.reshape(4, channels, 2 * width)
        total = pre[0] + pre[1] + pre[2] + pre[3]
        for h in range(2):
            whole = (total[:, h * width : (h + 1) * width] + enc[row + h].astype(F32)).astype(BF16)
            joined[row + h] = whole
            put3(row + h + 1, whole)

    nothing = jnp.zeros((PAD, BIG * inner, width), BF16)

    @pl.when(above)
    def _():
        down(h_args[1], *h_args[2:]).wait_recv()
        put11(0, h_halo[0])

    @pl.when(jnp.logical_not(above))
    def _():
        s11[0:PAD] = nothing

    @pl.when(below)
    def _():
        up(h_args[0], *h_args[2:]).wait_recv()
        put11(rows + PAD, h_halo[1])

    @pl.when(jnp.logical_not(below))
    def _():
        s11[rows + PAD : rows + 2 * PAD] = nothing

    @pl.loop(0, 2)
    def _(side):
        mixed(side * (rows - 2))

    j_args = (joined.at[0], joined.at[rows - 1], j_halo, j_send, j_recv)
    edges_start(*j_args)

    @pl.loop(1, rows // 2 - 1)
    def _(pair):
        mixed(2 * pair)

    def decode(row):
        d = conv3(w3d, dec_col, row)
        for h in range(2):
            out[row + h] = d[:, h * width : (h + 1) * width]

    @pl.loop(1, rows // 2 - 1)
    def _(pair):
        decode(2 * pair)

    edges3(*j_args)
    decode(0)
    decode(rows - 2)

    edges_sent(*x_args)
    edges_sent(*h_args)
    edges_sent(*j_args)
    for chunk in range(len(chunks)):
        for step in range(1, frames):
            share(step, chunk).wait_send()


def per_device(
    frames,
    spaces,
    features,
    enc_w,
    enc_b,
    mix_w,
    mix_b,
    branch3,
    branch5,
    branch7,
    branch11,
    branch_b,
    dec_w,
    dec_b,
):
    channels, rows, width = features.shape[1:]
    inner = mix_w.shape[0] // GROUPS
    branches = [jnp.transpose(w, (0, 1, 3, 2)) for w in (branch3, branch5, branch7, branch11)]
    vmem = pl.BlockSpec(memory_space=pltpu.VMEM)
    hbm = pl.BlockSpec(memory_space=pltpu.HBM)
    strip = (rows, channels, width)
    pair = pltpu.SemaphoreType.DMA((2,))
    many = pltpu.SemaphoreType.DMA((3 * (frames - 1),))
    decoded = pl.pallas_call(
        functools.partial(kernel, frames, spaces),
        out_shape=pltpu.VMEM(strip, BF16),
        in_specs=[hbm] * 8 + [vmem] * 4,
        out_specs=vmem,
        scratch_shapes=[
            pltpu.VMEM((channels, rows, width), BF16),
            pltpu.VMEM(strip, BF16),
            pltpu.VMEM(enc_w.shape, BF16),
            pltpu.VMEM((mix_w.shape[0], 128), BF16),
            pltpu.VMEM(dec_w.shape, BF16),
            pltpu.VMEM((BIG * BIG * inner, 4 * channels), BF16),
            pltpu.VMEM((channels, 9 * channels), BF16),
            pltpu.VMEM((channels, 9 * channels), BF16),
            pltpu.VMEM((4 * channels, BIG * BIG * inner), BF16),
            pltpu.VMEM(branches[0].shape, BF16),
            pltpu.VMEM(branches[1].shape, BF16),
            pltpu.VMEM(branches[2].shape, BF16),
            pltpu.VMEM(branches[3].shape, BF16),
            pltpu.VMEM((rows + 2, 3 * channels, width), BF16),
            pltpu.VMEM((rows + 2 * PAD, BIG * inner, width), BF16),
            pltpu.VMEM(strip, BF16),
            pltpu.VMEM((GROUPS, rows, inner, width), BF16),
            pltpu.VMEM((frames - 1, rows, inner, width), BF16),
            pltpu.VMEM((2, PAD, inner, width), BF16),
            pltpu.VMEM(strip, BF16),
            pltpu.VMEM((2, channels, width), BF16),
            pltpu.VMEM((2, PAD, inner, width), BF16),
            pltpu.VMEM((2, channels, width), BF16),
            pltpu.SemaphoreType.DMA((8,)),
            pair,
            pair,
            many,
            many,
            pair,
            pair,
            pair,
            pair,
        ],
        compiler_params=pltpu.CompilerParams(
            collective_id=0, has_side_effects=True, vmem_limit_bytes=62 * 2**20
        ),
    )(
        features,
        enc_w,
        mix_w,
        *branches,
        dec_w,
        enc_b[None],
        mix_b[None],
        branch_b,
        dec_b[None],
    )
    return jnp.transpose(decoded, (1, 0, 2))[None]


def solution(mesh):
    placed = (
        P("frame", None, "space", None),
        P(),
        P(),
        P(),
        P(),
        P(None, None, "frame", None),
        P(None, None, "frame", None),
        P(None, None, "frame", None),
        P(None, None, "frame", None),
        P(None, "frame"),
        P(),
        P(),
    )
    return jax.shard_map(
        functools.partial(per_device, mesh.shape["frame"], mesh.shape["space"]),
        mesh=mesh,
        in_specs=placed,
        out_specs=P("frame", None, "space", None),
        check_vma=False,
    )
```
